32 devices in a mesh: chan: 8 (over z, y), tm: 4 (over x, core).
Axes of the slice: x: 2, y: 2, z: 4, core: 2. Of those that a mesh axis runs over, the one named last changes fastest.
Arguments:
- visibilities: bfloat16 [16, 16, 2, 512, 512], P('chan', 'tm'), may hold values from -640 to 640, as said below
- model: bfloat16 [16, 16, 2, 512, 512], P('chan', 'tm'), may hold values from -32 to 32, as said below
- beam_left: bfloat16 [8, 256, 128], replicated, may hold values from -0.5 to 0.5
- beam_right: bfloat16 [8, 256, 128], replicated, may hold values from -0.0234375 to 0.0234375
- weight_index: int32 [16, 16], P('chan'), may hold values from 0 to 7
- target_bank: int32 [16, 16, 16], P('chan', 'tm'), may hold values from 0 to 7
- widths: int32 [16], P('chan'), may hold values from 0 to 2, as said below
Outputs:
- covariance: float32 [4096, 256], P('chan')
The draws below stay inside these ranges and needn't reach their ends.
Inputs may be any that keep to these rules, and one draw needn't show every extreme that they name: `visibilities`: real part at index 0 and imaginary part at index 1; each matrix is Hermitian in its last two dimensions. `model`: real part at index 0 and imaginary part at index 1; each matrix is Hermitian in its last two dimensions. `widths`: some channel has width 2.
All inputs are finite; a program needn't handle non-finite values.
Results may differ from the reference program's by a relative error of at most 0.0041.
Values sent between devices are 32-bit elements; how exact they have to be, the bound alone decides.
No kernel may reach another device: no remote copies, remote signals or barrier semaphores. Data moves between devices by JAX's collectives and lax.ppermute only.
A program may use at most 256 MiB of HBM per device.

```python
import math
import jax
import jax.numpy as jnp
from jax import lax

N = 512
BLK = 128
BEAMS = 256
BANKS = 8
NWEIGHT = 8
ITERS = 6
HW = 2
CHANNELS = 16
INTERVALS = 16
NBLK = 16


def joint_draw(key):
    keys = jax.random.split(key, 9)
    shape = (CHANNELS, INTERVALS, N, N)
    raw_re = jax.random.truncated_normal(keys[0], -4.0, 4.0, shape, jnp.float32)
    raw_im = jax.random.truncated_normal(keys[1], -4.0, 4.0, shape, jnp.float32)
    mod_re = 0.5 * (raw_re + jnp.swapaxes(raw_re, -1, -2))
    mod_im = 0.5 * (raw_im - jnp.swapaxes(raw_im, -1, -2))
    base_amp = jnp.exp(jax.random.uniform(keys[3], (CHANNELS, 1, N), jnp.float32, math.log(0.5), math.log(2.0)))
    amplitude = base_amp * jnp.exp(0.15 * jax.random.truncated_normal(keys[4], -4.0, 4.0, (CHANNELS, INTERVALS, N), jnp.float32))
    phase = jax.random.uniform(keys[5], (CHANNELS, 1, N), jnp.float32, -math.pi, math.pi)
    phase = phase + 0.3 * jax.random.truncated_normal(keys[6], -4.0, 4.0, (CHANNELS, INTERVALS, N), jnp.float32)
    gain_re = amplitude * jnp.cos(phase)
    gain_im = amplitude * jnp.sin(phase)
    noise_re = 0.1 * jax.random.truncated_normal(keys[7], -4.0, 4.0, shape, jnp.float32)
    noise_im = 0.1 * jax.random.truncated_normal(keys[8], -4.0, 4.0, shape, jnp.float32)
    noise_re = noise_re + jnp.swapaxes(noise_re, -1, -2)
    noise_im = noise_im - jnp.swapaxes(noise_im, -1, -2)
    left_re = gain_re[..., :, None] * mod_re - gain_im[..., :, None] * mod_im
    left_im = gain_re[..., :, None] * mod_im + gain_im[..., :, None] * mod_re
    vis_re = left_re * gain_re[..., None, :] + left_im * gain_im[..., None, :] + noise_re
    vis_im = left_im * gain_re[..., None, :] - left_re * gain_im[..., None, :] + noise_im
    model_pair = jnp.stack([mod_re, mod_im], axis=2)
    vis_pair = jnp.stack([vis_re, vis_im], axis=2)
    return (model_pair, vis_pair)


def draw_visibilities(key, part):
    model_pair, vis_pair = joint_draw(key)
    return vis_pair.astype(jnp.bfloat16)


def draw_model(key, part):
    model_pair, vis_pair = joint_draw(key)
    return model_pair.astype(jnp.bfloat16)


def draw_widths(key, part):
    key = jax.random.fold_in(key, 7)
    first_key, second_key = jax.random.split(key, 2)
    drawn = jax.random.randint(first_key, (CHANNELS,), 0, HW + 1, jnp.int32)
    chosen = jax.random.randint(second_key, (), 0, CHANNELS, jnp.int32)
    return jnp.where(jnp.arange(CHANNELS, dtype=jnp.int32) == chosen, HW, drawn).astype(jnp.int32)


def place_ends(values, stream_key, low, top_value):
    dims = values.shape
    spot = [jax.random.randint(jax.random.fold_in(stream_key, axis), (), 0, dims[axis]) for axis in range(len(dims))]
    values = values.at[tuple(spot)].set(low)
    longest = dims.index(max(dims))
    spot[longest] = (spot[longest] + 1) % dims[longest]
    return values.at[tuple(spot)].set(top_value)


def centred(rng, dims, scale, most, kind=jnp.bfloat16):
    entries = jax.random.normal(rng, dims, jnp.float32) * scale
    return jnp.minimum(jnp.maximum(entries, -most), most).astype(kind)


def setup_inputs(seed: int = 0) -> dict:
    streams_of = jax.random.split(jax.random.key(seed), 8)
    return {
        "visibilities": draw_visibilities(jax.random.fold_in(streams_of[7], 71), 0),
        "model": draw_model(jax.random.fold_in(streams_of[7], 71), 0),
        "beam_left": centred(streams_of[2], (NWEIGHT, BEAMS, BLK), BLK ** -0.5, 0.5),
        "beam_right": centred(streams_of[3], (NWEIGHT, BEAMS, BLK), (BLK * CHANNELS * INTERVALS * NBLK // BANKS) ** -0.5, 0.0234375),
        "weight_index": place_ends(jax.random.randint(streams_of[4], (CHANNELS, NBLK), 0, NWEIGHT), jax.random.fold_in(streams_of[4], 1), 0, NWEIGHT - 1).astype(jnp.int32),
        "target_bank": place_ends(jax.random.randint(streams_of[5], (CHANNELS, INTERVALS, NBLK), 0, BANKS), jax.random.fold_in(streams_of[5], 1), 0, BANKS - 1).astype(jnp.int32),
        "widths": draw_widths(jax.random.fold_in(streams_of[7], 71), 0),
    }


epsilon = 1e-06

def contract(vector, matrix):
    return jnp.einsum('...q,...qp->...p', vector, matrix, precision=lax.Precision.HIGHEST)

def stefcal(visibilities, model):
    vis_re = visibilities[..., 0, :, :].astype(jnp.float32)
    vis_im = visibilities[..., 1, :, :].astype(jnp.float32)
    mod_re = model[..., 0, :, :].astype(jnp.float32)
    mod_im = model[..., 1, :, :].astype(jnp.float32)
    cross_re = mod_re * vis_re + mod_im * vis_im
    cross_im = mod_im * vis_re - mod_re * vis_im
    power = mod_re * mod_re + mod_im * mod_im
    gain_re = jnp.ones(vis_re.shape[:-1], jnp.float32)
    gain_im = jnp.zeros(vis_re.shape[:-1], jnp.float32)
    for sweep_index in range(ITERS):
        num_re = contract(gain_re, cross_re) - contract(gain_im, cross_im)
        num_im = contract(gain_re, cross_im) + contract(gain_im, cross_re)
        denominator = contract(gain_re * gain_re + gain_im * gain_im, power) + epsilon
        new_re = num_re / denominator
        new_im = num_im / denominator
        if sweep_index % 2 == 1:
            gain_re = 0.5 * (new_re + gain_re)
            gain_im = 0.5 * (new_im + gain_im)
        else:
            gain_re = new_re
            gain_im = new_im
    return (gain_re, gain_im)

def align_phase(gain_re, gain_im):
    first_re = gain_re[..., :1]
    first_im = gain_im[..., :1]
    divisor = jnp.maximum(jnp.sqrt(first_re * first_re + first_im * first_im), 1.0)
    unit_re = first_re / divisor
    unit_im = -first_im / divisor
    return (gain_re * unit_re - gain_im * unit_im, gain_re * unit_im + gain_im * unit_re)

def calibrate(smooth_re, smooth_im, visibilities):
    vis_re = visibilities[..., 0, :, :].astype(jnp.float32)
    vis_im = visibilities[..., 1, :, :].astype(jnp.float32)
    denominator = jnp.maximum(smooth_re * smooth_re + smooth_im * smooth_im, 1.0)
    inv_re = smooth_re / denominator
    inv_im = -smooth_im / denominator
    row_re = inv_re[..., :, None]
    row_im = inv_im[..., :, None]
    col_re = inv_re[..., None, :]
    col_im = inv_im[..., None, :]
    left_re = row_re * vis_re - row_im * vis_im
    left_im = row_re * vis_im + row_im * vis_re
    out_re = left_re * col_re + left_im * col_im
    out_im = left_im * col_re - left_re * col_im
    return jnp.stack([out_re, out_im], axis=-3).astype(jnp.bfloat16)

def smooth_time(ref_re, ref_im, width):
    interval = jnp.arange(INTERVALS)
    padded_re = jnp.pad(ref_re, ((HW, HW), (0, 0)))
    padded_im = jnp.pad(ref_im, ((HW, HW), (0, 0)))
    summed_re = jnp.zeros_like(ref_re)
    summed_im = jnp.zeros_like(ref_im)
    counts = jnp.zeros((INTERVALS,), jnp.float32)
    for offset in range(-HW, HW + 1):
        inside = ((abs(offset) <= width) & (interval + offset >= 0) & (interval + offset < INTERVALS)).astype(jnp.float32)
        summed_re = summed_re + inside[:, None] * padded_re[HW + offset:HW + offset + INTERVALS]
        summed_im = summed_im + inside[:, None] * padded_im[HW + offset:HW + offset + INTERVALS]
        counts = counts + inside
    return (summed_re / counts[:, None], summed_im / counts[:, None])

def beam_channel(calibrated, left, right):
    group_count = N // BLK
    pieces = calibrated.astype(jnp.float32).reshape((-1, 2, group_count, BLK, group_count, BLK))
    left_groups = left.astype(jnp.float32).reshape((group_count, group_count, BEAMS, BLK))
    right_groups = right.astype(jnp.float32).reshape((group_count, group_count, BEAMS, BLK))
    formed = jnp.einsum('ijux,tsixjy->tijsuy', left_groups, pieces).astype(jnp.bfloat16)
    contrib = jnp.einsum('tijsuy,ijvy->tijsuv', formed.astype(jnp.float32), right_groups)
    return contrib.reshape((-1, 2, BEAMS, BEAMS))

def reference(visibilities, model, beam_left, beam_right, weight_index, target_bank, widths):

    def per_channel(accumulated, channel_data):
        vis_one, model_one, weight_one, banks_one, width_one = channel_data
        gain_re, gain_im = stefcal(vis_one, model_one)
        ref_re, ref_im = align_phase(gain_re, gain_im)
        smooth_re, smooth_im = smooth_time(ref_re, ref_im, width_one)
        calibrated = calibrate(smooth_re, smooth_im, vis_one)
        contrib = beam_channel(calibrated, beam_left[weight_one], beam_right[weight_one])
        accumulated = accumulated.at[banks_one.reshape(-1)].add(contrib)
        return (accumulated, None)
    start_banks = jnp.zeros((BANKS, 2, BEAMS, BEAMS), jnp.float32)
    final_banks, unused = lax.scan(per_channel, start_banks, (visibilities, model, weight_index, target_bank, widths))
    return final_banks.reshape((BANKS * 2 * BEAMS, BEAMS))
```

```python
import functools

import jax
import jax.numpy as jnp
from jax import lax
from jax.experimental import pallas as pl
from jax.experimental.pallas import tpu as pltpu
from jax.sharding import PartitionSpec as P

N = 512
BLK = 128
BEAMS = 256
BANKS = 8
NWEIGHT = 8
ITERS = 6
HW = 2
GROUPS = N // BLK
GAINS_VMEM = 52 * 1024 * 1024
PREPARE_VMEM = 16 * 1024 * 1024
CALIBRATE_VMEM = 40 * 1024 * 1024
PRODUCTS_VMEM = 24 * 1024 * 1024

epsilon = 1e-06


def split_bf16(value):
    high = value.astype(jnp.bfloat16)
    low = (value - high.astype(jnp.float32)).astype(jnp.bfloat16)
    return high, low


GROUP = 2


def gains_kernel(vis_hbm, mod_hbm, out_ref, vis, mod, *scratch, channels, intervals, rows):
    count = channels * intervals // GROUP
    matrices, powers, (first, arrived) = scratch[:count], scratch[count : 2 * count], scratch[2 * count :]
    zero = jnp.zeros((8, N), jnp.float32)

    def place(group, k):
        return divmod(group * GROUP + k, intervals)

    def fetch(group, k):
        c, t = place(group, k)
        return (
            pltpu.make_async_copy(vis_hbm.at[c, t], vis.at[c, t], arrived.at[0, c, t]),
            pltpu.make_async_copy(mod_hbm.at[c, t], mod.at[c, t], arrived.at[1, c, t]),
        )

    def request(group):
        for k in range(GROUP):
            for copy in fetch(group, k):
                copy.start()

    request(0)

    def build(group, k, start, sums):
        c, t = place(group, k)
        at = pl.ds(start, rows)
        vis_re = vis[c, t, 0, at, :].astype(jnp.float32)
        vis_im = vis[c, t, 1, at, :].astype(jnp.float32)
        mod_re = mod[c, t, 0, at, :].astype(jnp.float32)
        mod_im = mod[c, t, 1, at, :].astype(jnp.float32)
        parts = (
            mod_re * vis_re + mod_im * vis_im,
            mod_im * vis_re - mod_re * vis_im,
            mod_re * mod_re + mod_im * mod_im,
        )
        out = []
        for index, part in enumerate(parts):
            if index < 2:
                matrices[group][k, pl.ds(index * N + start, rows), :] = part.astype(jnp.bfloat16)
            else:
                powers[group][k, at, :] = part
            out.append(sums[index] + jnp.sum(part.reshape(rows // 8, 8, N), axis=0))
        return tuple(out)

    def first_gains(group, k, sums):
        num_re, num_im, power = (jnp.sum(part, axis=0, keepdims=True) for part in sums)
        power = power + epsilon
        first[group, k, 0:1, :] = num_re / power
        first[group, k, 1:2, :] = num_im / power

    def build_in_pieces(group):
        for k in range(GROUP):
            sums = (zero, zero, zero)
            for start in range(0, N, rows):
                sums = build(group, k, start, sums)
                if start + rows == N:
                    first_gains(group, k, sums)
                yield

    row = lax.broadcasted_iota(jnp.int32, (8, N), 0)

    def slab(*entries):
        value = jnp.zeros((8, N), jnp.float32)
        for position, entry in enumerate(entries):
            value = jnp.where(row == position, entry.astype(jnp.float32), value)
        return value.astype(jnp.bfloat16)

    def spread(gain_re, gain_im):
        magnitude = gain_re * gain_re + gain_im * gain_im
        return [
            jnp.broadcast_to(magnitude[:, i * BLK : (i + 1) * BLK], (BLK, BLK)).T for i in range(GROUPS)
        ]

    def products(group, k, gain, tiles):
        gain_re, gain_im = gain
        re_high, re_low = split_bf16(gain_re)
        im_high, im_low = split_bf16(gain_im)
        left = slab(re_high, re_low, im_high, im_low)
        right = slab(-im_high, -im_low, re_high, re_low)
        num = jnp.dot(
            jnp.concatenate([left, right], axis=1), matrices[group][k], preferred_element_type=jnp.float32
        )
        denominator = []
        for j in range(GROUPS):
            total = zero[:, :BLK]
            for i in range(GROUPS):
                block = powers[group][k, i * BLK : (i + 1) * BLK, j * BLK : (j + 1) * BLK]
                total = total + jnp.sum((block * tiles[i]).reshape(BLK // 8, 8, BLK), axis=0)
            denominator.append(jnp.sum(total, axis=0, keepdims=True))
        return num, jnp.concatenate(denominator, axis=1) + epsilon

    def update(index, gain, num, denominator):
        new_re = (num[0:1] + num[1:2]) / denominator
        new_im = (num[2:3] + num[3:4]) / denominator
        if index % 2 == 1:
            return 0.5 * (new_re + gain[0]), 0.5 * (new_im + gain[1])
        return new_re, new_im

    def iterate(group, beside):
        gains = [(first[group, k, 0:1, :], first[group, k, 1:2, :]) for k in range(GROUP)]
        tiles = [spread(*gain) for gain in gains]
        waiting = None
        for index in range(1, ITERS):
            for k in range(GROUP):
                found = products(group, k, gains[k], tiles[k])
                beside()
                if waiting is not None:
                    before, at, values = waiting
                    gains[at] = update(before, gains[at], *values)
                    tiles[at] = spread(*gains[at])
                waiting = (index, k, found)
        before, at, values = waiting
        gains[at] = update(before, gains[at], *values)
        return gains

    for k in range(GROUP):
        for copy in fetch(0, k):
            copy.wait()
        if k + 1 < count:
            request(k + 1)

        def chunk(index, sums, k=k):
            return build(0, k, pl.multiple_of(index * rows, rows), sums)

        first_gains(0, k, lax.fori_loop(0, N // rows, chunk, (zero, zero, zero), unroll=2))

    for group in range(count):
        later = iter(())
        if group + 1 < count:
            for k in range(GROUP):
                for copy in fetch(group + 1, k):
                    copy.wait()
            if group + 1 + GROUP < count:
                request(group + 1 + GROUP)
            later = build_in_pieces(group + 1)
        share = -(-(N // rows) // (ITERS - 1))

        def beside():
            for _ in range(share):
                next(later, None)

        for k, (gain_re, gain_im) in enumerate(iterate(group, beside)):
            c, t = place(group, k)
            first_re = gain_re[:, :1]
            first_im = gain_im[:, :1]
            divisor = jnp.maximum(jnp.sqrt(first_re * first_re + first_im * first_im), 1.0)
            unit_re = first_re / divisor
            unit_im = -first_im / divisor
            out_ref[c, t, 0:1, :] = gain_re * unit_re - gain_im * unit_im
            out_ref[c, t, 1:2, :] = gain_re * unit_im + gain_im * unit_re


def referenced_gains(visibilities, model):
    channels, intervals = visibilities.shape[:2]
    there = pl.BlockSpec(memory_space=pltpu.HBM)
    return pl.pallas_call(
        functools.partial(gains_kernel, channels=channels, intervals=intervals, rows=32),
        in_specs=[there, there],
        out_specs=pl.BlockSpec(memory_space=pltpu.VMEM),
        out_shape=jax.ShapeDtypeStruct((channels, intervals, 2, N), jnp.float32),
        scratch_shapes=[
            pltpu.VMEM(visibilities.shape, jnp.bfloat16),
            pltpu.VMEM(model.shape, jnp.bfloat16),
        ]
        + [pltpu.VMEM((GROUP, 2 * N, N), jnp.bfloat16)] * (channels * intervals // GROUP)
        + [pltpu.VMEM((GROUP, N, N), jnp.float32)] * (channels * intervals // GROUP)
        + [
            pltpu.VMEM((channels * intervals // GROUP, GROUP, 8, N), jnp.float32),
            pltpu.SemaphoreType.DMA((2, channels, intervals)),
        ],
        compiler_params=pltpu.CompilerParams(vmem_limit_bytes=GAINS_VMEM),
        cost_estimate=pl.CostEstimate(
            flops=channels * intervals * N * N * 60, bytes_accessed=channels * intervals * N * N * 8, transcendentals=0
        ),
        name="gains",
    )(visibilities, model)


ROWS = (96, 96, 64)


PIECE = 32
PIECES = BLK // PIECE
CELLS = 2 * PIECES


def prepare_kernel(right_ref, table):
    for w in range(NWEIGHT):
        table[w * BLK : (w + 1) * BLK, :] = right_ref[w].astype(jnp.float32).T.astype(jnp.bfloat16)


def calibrate_kernel(
    weight_ref, target_ref, width_ref, place_ref,
    vis_hbm, mid_ref, low_ref, high_ref, left_ref, table, *refs, channels, intervals, all_intervals,
):
    send, keep = refs[:2]
    own_cells, refs = refs[2 : 2 + CELLS], refs[2 + CELLS :]
    cells, refs = refs[:CELLS], refs[CELLS:]
    vis, inverse, down_even, down_odd, arrived = refs[:5]
    steps = channels * intervals

    def fetch(step):
        return pltpu.make_async_copy(
            vis_hbm.at[step // intervals, step % intervals], vis.at[step], arrived.at[step]
        )

    for step in range(2):
        fetch(step).start()

    def spread(at, down):
        for part in range(2):
            for i in range(GROUPS):
                span = slice(i * BLK, (i + 1) * BLK)
                down[part, span, :] = jnp.broadcast_to(inverse[at, part : part + 1, span], (BLK, BLK)).T

    for channel in range(channels):
        width = width_ref[channel]
        for interval in range(intervals):
            smooth = jnp.zeros((2, N), jnp.float32)
            count = jnp.float32(0)
            for offset in range(-HW, HW + 1):
                at = place_ref[0] + interval + offset
                inside = ((abs(offset) <= width) & (at >= 0) & (at < all_intervals)).astype(jnp.float32)
                spot = interval + offset
                if spot < 0:
                    value = low_ref[channel, spot + HW]
                elif spot >= intervals:
                    value = high_ref[channel, spot - intervals]
                else:
                    value = mid_ref[channel, spot]
                smooth = smooth + inside * value
                count = count + inside
            smooth = smooth / count
            squares = smooth * smooth
            denominator = jnp.maximum(squares[0:1] + squares[1:2], 1.0)
            at = channel * intervals + interval
            inverse[at, 0:1, :] = smooth[0:1] / denominator
            inverse[at, 1:2, :] = -smooth[1:2] / denominator
    for array in cells:
        array[...] = jnp.zeros_like(array)
    spread(0, down_even)

    def add_later(waiting):
        cell, piece, value_re, value_im = waiting
        cells[piece][cell] += value_re
        cells[PIECES + piece][cell] += value_im

    def calibrate(step, down, next_down):
        channel = step // intervals
        interval = step % intervals
        spread(jnp.minimum(step + 1, steps - 1), next_down)
        waiting = []
        for i in range(GROUPS):
            cell = [
                weight_ref[channel, block] * BANKS + target_ref[channel, interval * GROUPS * GROUPS + block]
                for block in range(i * GROUPS, (i + 1) * GROUPS)
            ]
            for j in range(GROUPS):
                span = slice(j * BLK, (j + 1) * BLK)
                for piece in range(PIECES):
                    at = slice(i * BLK + piece * PIECE, i * BLK + (piece + 1) * PIECE)
                    row_re = down[0, at, :]
                    row_im = down[1, at, :]
                    vis_re = vis[step, 0, at, span].astype(jnp.float32)
                    vis_im = vis[step, 1, at, span].astype(jnp.float32)
                    col_re = inverse[step, 0:1, span]
                    col_im = inverse[step, 1:2, span]
                    left_re = row_re * vis_re - row_im * vis_im
                    left_im = row_re * vis_im + row_im * vis_re
                    out_re = left_re * col_re + left_im * col_im
                    out_im = left_im * col_re - left_re * col_im
                    if len(waiting) == 2:
                        add_later(waiting.pop(0))
                    waiting.append((cell[j], piece, out_re, out_im))
        for entry in waiting:
            add_later(entry)

    def pair(turn, carry):
        step = 2 * turn
        fetch(step).wait()
        fetch(step + 1).wait()
        calibrate(step, down_even, down_odd)
        calibrate(step + 1, down_odd, down_even)
        return carry

    for step in range(2, steps):
        fetch(step).start()
    lax.fori_loop(0, steps // 2, pair, 0)
    four = BANKS // 2

    def cell_of(turn, w):
        own = w * BANKS + place_ref[3 + four + turn]
        for array, out in zip(cells, own_cells):
            out[w * four + turn] = array[own]
        return w * BANKS + place_ref[3 + turn]

    bank_products(place_ref, cells, cell_of, left_ref, table, send, keep, *refs[5:])


def own_products_kernel(place_ref, left_ref, table, *refs):
    def cell_of(turn, w):
        return w * (BANKS // 2) + turn

    bank_products(place_ref, refs[:CELLS], cell_of, left_ref, table, *refs[CELLS:])


def bank_products(
    place_ref, cells, cell_of, left_ref, table, send, keep, formed_even, formed_odd, product_even, product_odd
):
    count = BANKS // 2
    core = place_ref[1]
    across = place_ref[2]
    formed = (formed_even, formed_odd)
    product = (product_even, product_odd)

    def left_product(turn, w):
        cell = cell_of(turn, w)
        pair = jnp.concatenate(
            [
                jnp.concatenate([array[cell] for array in cells[:PIECES]], axis=0),
                jnp.concatenate([array[cell] for array in cells[PIECES:]], axis=0),
            ],
            axis=1,
        )
        high, low = split_bf16(pair)
        left = left_ref[w]
        beams = jnp.dot(
            jnp.concatenate([left, left], axis=1),
            jnp.concatenate([high, low], axis=0),
            preferred_element_type=jnp.float32,
        ).astype(jnp.bfloat16)
        formed[turn % 2][:BEAMS, w * BLK : (w + 1) * BLK] = beams[:, :BLK]
        formed[turn % 2][BEAMS:, w * BLK : (w + 1) * BLK] = beams[:, BLK:]

    def right_product(turn):
        product[turn % 2][...] = jnp.dot(
            formed[turn % 2][...], table[...], preferred_element_type=jnp.float32
        )

    def hand_out(turn):
        for part, out in ((1 - core, send), (core, keep)):
            start = 0
            for group, size in enumerate(rows // 2 for rows in ROWS):
                for away, half in ((0, across), (1, 1 - across)) if group < 2 else ((0, 0), (1, 1)):
                    at = part * BEAMS + start + half * size
                    out[turn, start + away * size : start + (away + 1) * size, :] = product[turn % 2][
                        pl.ds(pl.multiple_of(at, 16), size), :
                    ]
                start += 2 * size

    for turn in range(count + 1):
        if turn:
            right_product(turn - 1)
        if turn < count:
            for w in range(NWEIGHT):
                left_product(turn, w)
        if turn:
            hand_out(turn - 1)


SCALARS = pl.BlockSpec(memory_space=pltpu.SMEM)
VECTORS = pl.BlockSpec(memory_space=pltpu.VMEM)


def beam_products(weight_index, target_bank, widths, place, all_intervals, visibilities, mid, low, high, beam_left, beam_right):
    channels, intervals = visibilities.shape[:2]
    steps = channels * intervals
    table = pl.pallas_call(
        prepare_kernel,
        in_specs=[VECTORS],
        out_specs=VECTORS,
        out_shape=jax.ShapeDtypeStruct((NWEIGHT * BLK, BEAMS), jnp.bfloat16),
        compiler_params=pltpu.CompilerParams(vmem_limit_bytes=PREPARE_VMEM),
        cost_estimate=pl.CostEstimate(flops=10**6, bytes_accessed=1024 * 1024, transcendentals=0),
        name="prepare",
    )(lax.optimization_barrier((beam_right, mid))[0])
    banks_shape = [jax.ShapeDtypeStruct((BANKS // 2, BEAMS, BEAMS), jnp.float32)] * 2
    product_scratch = [pltpu.VMEM((2 * BEAMS, NWEIGHT * BLK), jnp.bfloat16)] * 2 + [
        pltpu.VMEM((2 * BEAMS, BEAMS), jnp.float32)
    ] * 2
    send_away, keep_away, *cells = pl.pallas_call(
        functools.partial(
            calibrate_kernel, channels=channels, intervals=intervals, all_intervals=all_intervals
        ),
        in_specs=[SCALARS] * 4 + [pl.BlockSpec(memory_space=pltpu.HBM)] + [VECTORS] * 5,
        out_specs=[VECTORS] * (2 + CELLS),
        scratch_shapes=[pltpu.VMEM((NWEIGHT * BANKS, PIECE, BLK), jnp.float32)] * CELLS
        + [
            pltpu.VMEM((steps, 2, N, N), jnp.bfloat16),
            pltpu.VMEM((steps, 8, N), jnp.float32),
            pltpu.VMEM((2, N, BLK), jnp.float32),
            pltpu.VMEM((2, N, BLK), jnp.float32),
            pltpu.SemaphoreType.DMA((steps,)),
        ]
        + product_scratch,
        out_shape=banks_shape
        + [jax.ShapeDtypeStruct((NWEIGHT * BANKS // 2, PIECE, BLK), jnp.float32)] * CELLS,
        compiler_params=pltpu.CompilerParams(vmem_limit_bytes=CALIBRATE_VMEM),
        cost_estimate=pl.CostEstimate(
            flops=2 * 10**9, bytes_accessed=steps * N * N * 8, transcendentals=0
        ),
        name="calibrate",
    )(
        weight_index, target_bank.reshape(channels, -1), widths, place,
        visibilities, mid, low, high, beam_left, table,
    )
    send_own, keep_own = pl.pallas_call(
        own_products_kernel,
        in_specs=[SCALARS] + [VECTORS] * (2 + CELLS),
        out_specs=[VECTORS] * 2,
        scratch_shapes=product_scratch,
        out_shape=banks_shape,
        compiler_params=pltpu.CompilerParams(vmem_limit_bytes=PRODUCTS_VMEM),
        cost_estimate=pl.CostEstimate(
            flops=2 * 10**9, bytes_accessed=2 * 1024 * 1024, transcendentals=0
        ),
        name="products",
    )(place, beam_left, table, *cells)
    return send_away, keep_away, send_own, keep_own


SLOTS = tuple((1 - (p >> 2)) | ((p & 3) << 1) for p in range(BANKS))


def swap(value, axis, mask):
    count = lax.axis_size(axis)
    return lax.ppermute(value, axis, [(i, i ^ mask) for i in range(count)])


def assemble_kernel(place_ref, mine, other, out, done):
    core = place_ref[1]
    across = place_ref[2]
    half_p, half_q = ROWS[0] // 2, ROWS[1] // 2
    copies = []
    for part, rows in ((core, mine), (1 - core, other)):
        base = part * BEAMS
        pieces = [
            (at + half * size, size)
            for half in (across, 1 - across)
            for at, size in ((0, half_p), (ROWS[0], half_q))
        ] + [(ROWS[0] + ROWS[1], ROWS[2])]
        start = 0
        for at, size in pieces:
            copies.append(
                pltpu.make_async_copy(
                    rows.at[start : start + size],
                    out.at[pl.ds(pl.multiple_of(base + at, 16), size)],
                    done.at[len(copies)],
                )
            )
            start += size
    for copy in copies:
        copy.start()
    for copy in copies:
        copy.wait()


def reduce_banks(place, send_away, keep_away, send_own, keep_own):
    four = BANKS // 2
    half_p, half_q = ROWS[0] // 2, ROWS[1] // 2
    q_at = 2 * half_p
    q_half = q_at + half_q
    r_at = q_half + half_q
    got_away = swap(send_away, "tm", 1)
    got_own = swap(send_own, "tm", 1)

    def away(low, high):
        return keep_away[:, low:high] + got_away[:, low:high]

    def own(low, high):
        return keep_own[:, low:high] + got_own[:, low:high]

    p_got = swap(away(0, q_at), "chan", 1)
    q_got = swap(jnp.concatenate([away(q_half, r_at), own(q_half, r_at)], axis=0), "tm", 2)
    r_here = jnp.stack([own(r_at, None), away(r_at, None)], axis=1)
    r_got = [swap(r_here[k], "chan", 2 * k) for k in (3, 2, 1)]
    p_here = own(0, q_at) + p_got
    p_got = swap(p_here[:, half_p:], "tm", 2)
    p_got, *r_got = lax.optimization_barrier((p_got, *r_got))
    p_here = p_here[:, :half_p] + p_got
    q_own = own(q_at, q_half) + q_got[four:]
    q_other = away(q_at, q_half) + q_got[:four]
    q_here = q_own + swap(q_other, "chan", 1)
    r_here = r_here[0] + r_got[0] + r_got[1] + r_got[2]
    r_here = r_here[0] + swap(r_here[1], "chan", 1)
    here = jnp.concatenate([p_here, q_here], axis=1)
    z_got = [swap(here[k], "chan", 2 * k) for k in (3, 2, 1)]
    here = here[0] + z_got[0] + z_got[1] + z_got[2]
    x_got = swap(jnp.concatenate([here, r_here], axis=0), "tm", 2)
    pq = half_p + half_q
    mine = jnp.concatenate([here, x_got[:pq], r_here + x_got[pq:]], axis=0)
    other = swap(mine, "tm", 1)
    return pl.pallas_call(
        assemble_kernel,
        in_specs=[SCALARS, VECTORS, VECTORS],
        out_specs=pl.BlockSpec(memory_space=pltpu.HBM),
        out_shape=jax.ShapeDtypeStruct((2 * BEAMS, BEAMS), jnp.float32),
        scratch_shapes=[pltpu.SemaphoreType.DMA((10,))],
        compiler_params=pltpu.CompilerParams(vmem_limit_bytes=PREPARE_VMEM),
        name="assemble",
    )(place, mine, other)


def reduce_plain(send_first, keep_first, send_last, keep_last):
    keep = jnp.concatenate([keep_first, keep_last])
    send = jnp.concatenate([send_first, send_last])
    banks = jnp.stack([keep, send], axis=1).reshape((BANKS * 2 * BEAMS, BEAMS))
    shares = lax.psum_scatter(banks, "chan", scatter_dimension=0, tiled=True)
    return lax.psum(shares, "tm")


def neighbour_gains(gains):
    count = lax.axis_size("tm")
    odd = lax.axis_index("tm") % 2 == 1
    head = gains[:, :HW]
    tail = gains[:, gains.shape[1] - HW :]
    inner = lax.ppermute(jnp.where(odd, head, tail), "tm", [(i, i ^ 1) for i in range(count)])
    links = [(i, i + 1) for i in range(1, count - 1, 2)]
    outer = lax.ppermute(jnp.where(odd, tail, head), "tm", links + [(j, i) for i, j in links])
    return jnp.where(odd, inner, outer), jnp.where(odd, outer, inner)


def local(visibilities, model, beam_left, beam_right, weight_index, target_bank, widths):
    local_intervals = visibilities.shape[1]
    count = lax.axis_size("tm")
    tm = lax.axis_index("tm")
    chan = lax.axis_index("chan")
    one_bank_each = lax.axis_size("chan") == BANKS and count == 4
    if one_bank_each:
        place = [tm * local_intervals, tm % 2, tm // 2] + [chan ^ slot for slot in SLOTS]
    else:
        place = [tm * local_intervals, 0, 0] + list(range(BANKS))
    place = jnp.stack([jnp.asarray(entry, jnp.int32) for entry in place])
    gains = referenced_gains(visibilities, model)
    low, high = neighbour_gains(gains)
    pieces = beam_products(
        weight_index, target_bank, widths, place, count * local_intervals,
        visibilities, gains, low, high, beam_left, beam_right,
    )
    if one_bank_each:
        return reduce_banks(place, *pieces)
    return reduce_plain(*pieces)


def solution(mesh):
    return jax.shard_map(
        local,
        mesh=mesh,
        in_specs=(
            P("chan", "tm", None, None, None),
            P("chan", "tm", None, None, None),
            P(),
            P(),
            P("chan", None),
            P("chan", "tm", None),
            P("chan"),
        ),
        out_specs=P("chan", None),
        check_vma=False,
    )
```

```python
import functools

import jax
import jax.numpy as jnp
from jax import lax
from jax.experimental import pallas as pl
from jax.experimental.pallas import tpu as pltpu
from jax.sharding import PartitionSpec as P

N = 512
BLK = 128
BEAMS = 256
BANKS = 8
NWEIGHT = 8
ITERS = 6
HW = 2
GROUPS = N // BLK
GAINS_VMEM = 52 * 1024 * 1024
PREPARE_VMEM = 16 * 1024 * 1024
CALIBRATE_VMEM = 40 * 1024 * 1024
PRODUCTS_VMEM = 24 * 1024 * 1024

epsilon = 1e-06


def split_bf16(value):
    high = value.astype(jnp.bfloat16)
    low = (value - high.astype(jnp.float32)).astype(jnp.bfloat16)
    return high, low


GROUP = 2


def gains_kernel(vis_hbm, mod_hbm, out_ref, vis, mod, *scratch, channels, intervals, rows):
    count = channels * intervals // GROUP
    matrices, powers, (first, arrived) = scratch[:count], scratch[count : 2 * count], scratch[2 * count :]
    zero = jnp.zeros((8, N), jnp.float32)

    def place(group, k):
        return divmod(group * GROUP + k, intervals)

    def fetch(group, k):
        c, t = place(group, k)
        return (
            pltpu.make_async_copy(vis_hbm.at[c, t], vis.at[c, t], arrived.at[0, c, t]),
            pltpu.make_async_copy(mod_hbm.at[c, t], mod.at[c, t], arrived.at[1, c, t]),
        )

    for group in range(count):
        for k in range(GROUP):
            for copy in fetch(group, k):
                copy.start()

    def build(group, k, start, sums):
        c, t = place(group, k)
        at = pl.ds(start, rows)
        vis_re = vis[c, t, 0, at, :].astype(jnp.float32)
        vis_im = vis[c, t, 1, at, :].astype(jnp.float32)
        mod_re = mod[c, t, 0, at, :].astype(jnp.float32)
        mod_im = mod[c, t, 1, at, :].astype(jnp.float32)
        parts = (
            mod_re * vis_re + mod_im * vis_im,
            mod_im * vis_re - mod_re * vis_im,
            mod_re * mod_re + mod_im * mod_im,
        )
        out = []
        for index, part in enumerate(parts):
            if index < 2:
                matrices[group][k, pl.ds(index * N + start, rows), :] = part.astype(jnp.bfloat16)
            else:
                powers[group][k, at, :] = part
            out.append(sums[index] + jnp.sum(part.reshape(rows // 8, 8, N), axis=0))
        return tuple(out)

    def first_gains(group, k, sums):
        num_re, num_im, power = (jnp.sum(part, axis=0, keepdims=True) for part in sums)
        power = power + epsilon
        first[group, k, 0:1, :] = num_re / power
        first[group, k, 1:2, :] = num_im / power

    def build_in_pieces(group):
        for k in range(GROUP):
            sums = (zero, zero, zero)
            for start in range(0, N, rows):
                sums = build(group, k, start, sums)
                if start + rows == N:
                    first_gains(group, k, sums)
                yield

    row = lax.broadcasted_iota(jnp.int32, (8, N), 0)

    def slab(*entries):
        value = jnp.zeros((8, N), jnp.float32)
        for position, entry in enumerate(entries):
            value = jnp.where(row == position, entry.astype(jnp.float32), value)
        return value.astype(jnp.bfloat16)

    def spread(gain_re, gain_im):
        magnitude = gain_re * gain_re + gain_im * gain_im
        return [
            jnp.broadcast_to(magnitude[:, i * BLK : (i + 1) * BLK], (BLK, BLK)).T for i in range(GROUPS)
        ]

    def products(group, k, gain, tiles):
        gain_re, gain_im = gain
        re_high, re_low = split_bf16(gain_re)
        im_high, im_low = split_bf16(gain_im)
        left = slab(re_high, re_low, im_high, im_low)
        right = slab(-im_high, -im_low, re_high, re_low)
        num = jnp.dot(
            jnp.concatenate([left, right], axis=1), matrices[group][k], preferred_element_type=jnp.float32
        )
        denominator = []
        for j in range(GROUPS):
            total = zero[:, :BLK]
            for i in range(GROUPS):
                block = powers[group][k, i * BLK : (i + 1) * BLK, j * BLK : (j + 1) * BLK]
                total = total + jnp.sum((block * tiles[i]).reshape(BLK // 8, 8, BLK), axis=0)
            denominator.append(jnp.sum(total, axis=0, keepdims=True))
        return num, jnp.concatenate(denominator, axis=1) + epsilon

    def update(index, gain, num, denominator):
        new_re = (num[0:1] + num[1:2]) / denominator
        new_im = (num[2:3] + num[3:4]) / denominator
        if index % 2 == 1:
            return 0.5 * (new_re + gain[0]), 0.5 * (new_im + gain[1])
        return new_re, new_im

    def iterate(group, beside):
        gains = [(first[group, k, 0:1, :], first[group, k, 1:2, :]) for k in range(GROUP)]
        tiles = [spread(*gain) for gain in gains]
        waiting = None
        for index in range(1, ITERS):
            for k in range(GROUP):
                found = products(group, k, gains[k], tiles[k])
                beside()
                if waiting is not None:
                    before, at, values = waiting
                    gains[at] = update(before, gains[at], *values)
                    tiles[at] = spread(*gains[at])
                waiting = (index, k, found)
        before, at, values = waiting
        gains[at] = update(before, gains[at], *values)
        return gains

    for k in range(GROUP):
        for copy in fetch(0, k):
            copy.wait()

        def chunk(index, sums, k=k):
            return build(0, k, pl.multiple_of(index * rows, rows), sums)

        first_gains(0, k, lax.fori_loop(0, N // rows, chunk, (zero, zero, zero), unroll=2))

    for group in range(count):
        later = iter(())
        if group + 1 < count:
            for k in range(GROUP):
                for copy in fetch(group + 1, k):
                    copy.wait()
            later = build_in_pieces(group + 1)
        share = -(-(N // rows) // (ITERS - 1))

        def beside():
            for _ in range(share):
                next(later, None)

        for k, (gain_re, gain_im) in enumerate(iterate(group, beside)):
            c, t = place(group, k)
            first_re = gain_re[:, :1]
            first_im = gain_im[:, :1]
            divisor = jnp.maximum(jnp.sqrt(first_re * first_re + first_im * first_im), 1.0)
            unit_re = first_re / divisor
            unit_im = -first_im / divisor
            out_ref[c, t, 0:1, :] = gain_re * unit_re - gain_im * unit_im
            out_ref[c, t, 1:2, :] = gain_re * unit_im + gain_im * unit_re


def referenced_gains(visibilities, model):
    channels, intervals = visibilities.shape[:2]
    there = pl.BlockSpec(memory_space=pltpu.HBM)
    return pl.pallas_call(
        functools.partial(gains_kernel, channels=channels, intervals=intervals, rows=32),
        in_specs=[there, there],
        out_specs=pl.BlockSpec(memory_space=pltpu.VMEM),
        out_shape=jax.ShapeDtypeStruct((channels, intervals, 2, N), jnp.float32),
        scratch_shapes=[
            pltpu.VMEM(visibilities.shape, jnp.bfloat16),
            pltpu.VMEM(model.shape, jnp.bfloat16),
        ]
        + [pltpu.VMEM((GROUP, 2 * N, N), jnp.bfloat16)] * (channels * intervals // GROUP)
        + [pltpu.VMEM((GROUP, N, N), jnp.float32)] * (channels * intervals // GROUP)
        + [
            pltpu.VMEM((channels * intervals // GROUP, GROUP, 8, N), jnp.float32),
            pltpu.SemaphoreType.DMA((2, channels, intervals)),
        ],
        compiler_params=pltpu.CompilerParams(vmem_limit_bytes=GAINS_VMEM),
        cost_estimate=pl.CostEstimate(
            flops=channels * intervals * N * N * 60, bytes_accessed=channels * intervals * N * N * 8, transcendentals=0
        ),
        name="gains",
    )(visibilities, model)


ROWS = (96, 96, 64)


PIECE = 32
PIECES = BLK // PIECE
CELLS = 2 * PIECES


def prepare_kernel(right_ref, table):
    for w in range(NWEIGHT):
        table[w * BLK : (w + 1) * BLK, :] = right_ref[w].astype(jnp.float32).T.astype(jnp.bfloat16)


def calibrate_kernel(
    weight_ref, target_ref, width_ref, place_ref,
    vis_hbm, mid_ref, low_ref, high_ref, left_ref, table, *refs, channels, intervals, all_intervals,
):
    send, keep = refs[:2]
    own_cells, refs = refs[2 : 2 + CELLS], refs[2 + CELLS :]
    cells, refs = refs[:CELLS], refs[CELLS:]
    vis, down_lines, along_lines, factors_even, factors_odd, arrived = refs[:6]
    steps = channels * intervals

    def fetch(step):
        return pltpu.make_async_copy(
            vis_hbm.at[step // intervals, step % intervals], vis.at[step], arrived.at[step]
        )

    for step in range(steps):
        fetch(step).start()

    def factor(at, factors, i):
        span = slice(i * (N // 2), (i + 1) * (N // 2))
        factors[span, :] = jnp.dot(
            down_lines[at, :, span].T.astype(jnp.bfloat16),
            along_lines[at].astype(jnp.bfloat16),
            preferred_element_type=jnp.float32,
        )

    down_lines[...] = jnp.zeros_like(down_lines)
    along_lines[...] = jnp.zeros_like(along_lines)
    for channel in range(channels):
        width = width_ref[channel]
        for interval in range(intervals):
            smooth = jnp.zeros((2, N), jnp.float32)
            count = jnp.float32(0)
            for offset in range(-HW, HW + 1):
                at = place_ref[0] + interval + offset
                inside = ((abs(offset) <= width) & (at >= 0) & (at < all_intervals)).astype(jnp.float32)
                spot = interval + offset
                if spot < 0:
                    value = low_ref[channel, spot + HW]
                elif spot >= intervals:
                    value = high_ref[channel, spot - intervals]
                else:
                    value = mid_ref[channel, spot]
                smooth = smooth + inside * value
                count = count + inside
            smooth = smooth / count
            squares = smooth * smooth
            inverse = smooth / jnp.maximum(squares[0:1] + squares[1:2], 1.0)
            high = inverse.astype(jnp.bfloat16).astype(jnp.float32)
            low = inverse - high
            re_high, im_high = high[0:1], -high[1:2]
            re_low, im_low = low[0:1], -low[1:2]
            at = channel * intervals + interval
            down = (re_high, re_high, re_low, im_high, im_high, im_low)
            along_re = (re_high, re_low, re_high, im_high, im_low, im_high)
            along_im = (-im_high, -im_low, -im_high, re_high, re_low, re_high)
            for k in range(6):
                down_lines[at, k : k + 1, :] = down[k]
                along_lines[at, k : k + 1, :N] = along_re[k]
                along_lines[at, k : k + 1, N:] = along_im[k]
    for i in range(2):
        factor(0, factors_even, i)

    for array in cells:
        array[...] = jnp.zeros_like(array)

    def add_later(waiting):
        cell, piece, value_re, value_im = waiting
        cells[piece][cell] += value_re
        cells[PIECES + piece][cell] += value_im

    def calibrate(step, factors, next_factors):
        channel = step // intervals
        interval = step % intervals
        waiting = []
        for i in range(GROUPS):
            if i % 2 == 0:
                factor(jnp.minimum(step + 1, steps - 1), next_factors, i // 2)
            for j in range(GROUPS):
                block = i * GROUPS + j
                cell = weight_ref[channel, block] * BANKS + target_ref[channel, interval * GROUPS * GROUPS + block]
                span = slice(j * BLK, (j + 1) * BLK)
                for piece in range(PIECES):
                    at = slice(i * BLK + piece * PIECE, i * BLK + (piece + 1) * PIECE)
                    vis_re = vis[step, 0, at, span].astype(jnp.float32)
                    vis_im = vis[step, 1, at, span].astype(jnp.float32)
                    fac_re = factors[at, span]
                    fac_im = factors[at, N + j * BLK : N + (j + 1) * BLK]
                    out_re = fac_re * vis_re - fac_im * vis_im
                    out_im = fac_re * vis_im + fac_im * vis_re
                    if len(waiting) == 2:
                        add_later(waiting.pop(0))
                    waiting.append((cell, piece, out_re, out_im))
        for entry in waiting:
            add_later(entry)

    def pair(turn, carry):
        step = 2 * turn
        fetch(step).wait()
        fetch(step + 1).wait()
        calibrate(step, factors_even, factors_odd)
        calibrate(step + 1, factors_odd, factors_even)
        return carry

    lax.fori_loop(0, steps // 2, pair, 0)
    four = BANKS // 2

    def cell_of(turn, w):
        own = w * BANKS + place_ref[3 + four + turn]
        for array, out in zip(cells, own_cells):
            out[w * four + turn] = array[own]
        return w * BANKS + place_ref[3 + turn]

    bank_products(place_ref, cells, cell_of, left_ref, table, send, keep, *refs[6:])


def own_products_kernel(place_ref, left_ref, table, *refs):
    def cell_of(turn, w):
        return w * (BANKS // 2) + turn

    bank_products(place_ref, refs[:CELLS], cell_of, left_ref, table, *refs[CELLS:])


def bank_products(
    place_ref, cells, cell_of, left_ref, table, send, keep, formed_even, formed_odd, product_even, product_odd
):
    count = BANKS // 2
    core = place_ref[1]
    across = place_ref[2]
    formed = (formed_even, formed_odd)
    product = (product_even, product_odd)

    def left_product(turn, w):
        cell = cell_of(turn, w)
        pair = jnp.concatenate(
            [
                jnp.concatenate([array[cell] for array in cells[:PIECES]], axis=0),
                jnp.concatenate([array[cell] for array in cells[PIECES:]], axis=0),
            ],
            axis=1,
        )
        high, low = split_bf16(pair)
        left = left_ref[w]
        beams = jnp.dot(
            jnp.concatenate([left, left], axis=1),
            jnp.concatenate([high, low], axis=0),
            preferred_element_type=jnp.float32,
        ).astype(jnp.bfloat16)
        formed[turn % 2][:BEAMS, w * BLK : (w + 1) * BLK] = beams[:, :BLK]
        formed[turn % 2][BEAMS:, w * BLK : (w + 1) * BLK] = beams[:, BLK:]

    def right_product(turn):
        product[turn % 2][...] = jnp.dot(
            formed[turn % 2][...], table[...], preferred_element_type=jnp.float32
        )

    def hand_out(turn):
        for part, out in ((1 - core, send), (core, keep)):
            start = 0
            for group, size in enumerate(rows // 2 for rows in ROWS):
                for away, half in ((0, across), (1, 1 - across)) if group < 2 else ((0, 0), (1, 1)):
                    at = part * BEAMS + start + half * size
                    out[turn, start + away * size : start + (away + 1) * size, :] = product[turn % 2][
                        pl.ds(pl.multiple_of(at, 16), size), :
                    ]
                start += 2 * size

    for turn in range(count + 1):
        if turn:
            right_product(turn - 1)
        if turn < count:
            for w in range(NWEIGHT):
                left_product(turn, w)
        if turn:
            hand_out(turn - 1)


SCALARS = pl.BlockSpec(memory_space=pltpu.SMEM)
VECTORS = pl.BlockSpec(memory_space=pltpu.VMEM)


def beam_products(weight_index, target_bank, widths, place, all_intervals, visibilities, mid, low, high, beam_left, beam_right):
    channels, intervals = visibilities.shape[:2]
    steps = channels * intervals
    table = pl.pallas_call(
        prepare_kernel,
        in_specs=[VECTORS],
        out_specs=VECTORS,
        out_shape=jax.ShapeDtypeStruct((NWEIGHT * BLK, BEAMS), jnp.bfloat16),
        compiler_params=pltpu.CompilerParams(vmem_limit_bytes=PREPARE_VMEM),
        cost_estimate=pl.CostEstimate(flops=10**6, bytes_accessed=1024 * 1024, transcendentals=0),
        name="prepare",
    )(lax.optimization_barrier((beam_right, mid))[0])
    banks_shape = [jax.ShapeDtypeStruct((BANKS // 2, BEAMS, BEAMS), jnp.float32)] * 2
    product_scratch = [pltpu.VMEM((2 * BEAMS, NWEIGHT * BLK), jnp.bfloat16)] * 2 + [
        pltpu.VMEM((2 * BEAMS, BEAMS), jnp.float32)
    ] * 2
    send_away, keep_away, *cells = pl.pallas_call(
        functools.partial(
            calibrate_kernel, channels=channels, intervals=intervals, all_intervals=all_intervals
        ),
        in_specs=[SCALARS] * 4 + [pl.BlockSpec(memory_space=pltpu.HBM)] + [VECTORS] * 5,
        out_specs=[VECTORS] * (2 + CELLS),
        scratch_shapes=[pltpu.VMEM((NWEIGHT * BANKS, PIECE, BLK), jnp.float32)] * CELLS
        + [
            pltpu.VMEM((steps, 2, N, N), jnp.bfloat16),
            pltpu.VMEM((steps, 16, N), jnp.float32),
            pltpu.VMEM((steps, 16, 2 * N), jnp.float32),
            pltpu.VMEM((N, 2 * N), jnp.float32),
            pltpu.VMEM((N, 2 * N), jnp.float32),
            pltpu.SemaphoreType.DMA((steps,)),
        ]
        + product_scratch,
        out_shape=banks_shape
        + [jax.ShapeDtypeStruct((NWEIGHT * BANKS // 2, PIECE, BLK), jnp.float32)] * CELLS,
        compiler_params=pltpu.CompilerParams(vmem_limit_bytes=CALIBRATE_VMEM),
        cost_estimate=pl.CostEstimate(
            flops=2 * 10**9, bytes_accessed=steps * N * N * 8, transcendentals=0
        ),
        name="calibrate",
    )(
        weight_index, target_bank.reshape(channels, -1), widths, place,
        visibilities, mid, low, high, beam_left, table,
    )
    send_own, keep_own = pl.pallas_call(
        own_products_kernel,
        in_specs=[SCALARS] + [VECTORS] * (2 + CELLS),
        out_specs=[VECTORS] * 2,
        scratch_shapes=product_scratch,
        out_shape=banks_shape,
        compiler_params=pltpu.CompilerParams(vmem_limit_bytes=PRODUCTS_VMEM),
        cost_estimate=pl.CostEstimate(
            flops=2 * 10**9, bytes_accessed=2 * 1024 * 1024, transcendentals=0
        ),
        name="products",
    )(place, beam_left, table, *cells)
    return send_away, keep_away, send_own, keep_own


SLOTS = tuple((1 - (p >> 2)) | ((p & 3) << 1) for p in range(BANKS))


def swap(value, axis, mask):
    count = lax.axis_size(axis)
    return lax.ppermute(value, axis, [(i, i ^ mask) for i in range(count)])


def assemble_kernel(place_ref, mine, other, out):
    core = place_ref[1]
    across = place_ref[2]
    half_p, half_q = ROWS[0] // 2, ROWS[1] // 2
    for part, rows in ((core, mine), (1 - core, other)):
        base = part * BEAMS
        start = 0
        for half in (across, 1 - across):
            for at, size in ((0, half_p), (ROWS[0], half_q)):
                out[pl.ds(pl.multiple_of(base + at + half * size, 16), size), :] = rows[start : start + size, :]
                start += size
        out[pl.ds(pl.multiple_of(base + start, 16), ROWS[2]), :] = rows[start:, :]


def reduce_banks(place, send_away, keep_away, send_own, keep_own):
    four = BANKS // 2
    half_p, half_q = ROWS[0] // 2, ROWS[1] // 2
    q_at = 2 * half_p
    q_half = q_at + half_q
    r_at = q_half + half_q
    got_away = swap(send_away, "tm", 1)
    got_own = swap(send_own, "tm", 1)

    def away(low, high):
        return keep_away[:, low:high] + got_away[:, low:high]

    def own(low, high):
        return keep_own[:, low:high] + got_own[:, low:high]

    p_got = swap(away(0, q_at), "chan", 1)
    q_got = swap(jnp.concatenate([away(q_half, r_at), own(q_half, r_at)], axis=0), "tm", 2)
    r_here = jnp.stack([own(r_at, None), away(r_at, None)], axis=1)
    r_got = [swap(r_here[k], "chan", 2 * k) for k in (3, 2, 1)]
    p_here = own(0, q_at) + p_got
    p_got = swap(p_here[:, half_p:], "tm", 2)
    p_got, *r_got = lax.optimization_barrier((p_got, *r_got))
    p_here = p_here[:, :half_p] + p_got
    q_own = own(q_at, q_half) + q_got[four:]
    q_other = away(q_at, q_half) + q_got[:four]
    q_here = q_own + swap(q_other, "chan", 1)
    r_here = r_here[0] + r_got[0] + r_got[1] + r_got[2]
    r_here = r_here[0] + swap(r_here[1], "chan", 1)
    here = jnp.concatenate([p_here, q_here], axis=1)
    z_got = [swap(here[k], "chan", 2 * k) for k in (3, 2, 1)]
    r_got = swap(r_here, "tm", 2)
    r_got, *z_got = lax.optimization_barrier((r_got, *z_got))
    here = here[0] + z_got[0] + z_got[1] + z_got[2]
    r_here = r_here + r_got
    mine = jnp.concatenate([here, swap(here, "tm", 2), r_here], axis=0)
    other = swap(mine, "tm", 1)
    return pl.pallas_call(
        assemble_kernel,
        in_specs=[SCALARS, VECTORS, VECTORS],
        out_specs=VECTORS,
        out_shape=jax.ShapeDtypeStruct((2 * BEAMS, BEAMS), jnp.float32),
        compiler_params=pltpu.CompilerParams(vmem_limit_bytes=PREPARE_VMEM),
        name="assemble",
    )(place, mine, other)


def reduce_plain(send_first, keep_first, send_last, keep_last):
    keep = jnp.concatenate([keep_first, keep_last])
    send = jnp.concatenate([send_first, send_last])
    banks = jnp.stack([keep, send], axis=1).reshape((BANKS * 2 * BEAMS, BEAMS))
    shares = lax.psum_scatter(banks, "chan", scatter_dimension=0, tiled=True)
    return lax.psum(shares, "tm")


def neighbour_gains(gains):
    count = lax.axis_size("tm")
    odd = lax.axis_index("tm") % 2 == 1
    head = gains[:, :HW]
    tail = gains[:, gains.shape[1] - HW :]
    inner = lax.ppermute(jnp.where(odd, head, tail), "tm", [(i, i ^ 1) for i in range(count)])
    links = [(i, i + 1) for i in range(1, count - 1, 2)]
    outer = lax.ppermute(jnp.where(odd, tail, head), "tm", links + [(j, i) for i, j in links])
    return jnp.where(odd, inner, outer), jnp.where(odd, outer, inner)


def local(visibilities, model, beam_left, beam_right, weight_index, target_bank, widths):
    local_intervals = visibilities.shape[1]
    count = lax.axis_size("tm")
    tm = lax.axis_index("tm")
    chan = lax.axis_index("chan")
    one_bank_each = lax.axis_size("chan") == BANKS and count == 4
    if one_bank_each:
        place = [tm * local_intervals, tm % 2, tm // 2] + [chan ^ slot for slot in SLOTS]
    else:
        place = [tm * local_intervals, 0, 0] + list(range(BANKS))
    place = jnp.stack([jnp.asarray(entry, jnp.int32) for entry in place])
    gains = referenced_gains(visibilities, model)
    low, high = neighbour_gains(gains)
    pieces = beam_products(
        weight_index, target_bank, widths, place, count * local_intervals,
        visibilities, gains, low, high, beam_left, beam_right,
    )
    if one_bank_each:
        return reduce_banks(place, *pieces)
    return reduce_plain(*pieces)


def solution(mesh):
    return jax.shard_map(
        local,
        mesh=mesh,
        in_specs=(
            P("chan", "tm", None, None, None),
            P("chan", "tm", None, None, None),
            P(),
            P(),
            P("chan", None),
            P("chan", "tm", None),
            P("chan"),
        ),
        out_specs=P("chan", None),
        check_vma=False,
    )
```

```python
import functools

import jax
import jax.numpy as jnp
from jax import lax
from jax.experimental import pallas as pl
from jax.experimental.pallas import tpu as pltpu
from jax.sharding import PartitionSpec as P

N = 512
BLK = 128
BEAMS = 256
BANKS = 8
NWEIGHT = 8
ITERS = 6
HW = 2
GROUPS = N // BLK
GAINS_VMEM = 52 * 1024 * 1024
PREPARE_VMEM = 16 * 1024 * 1024
CALIBRATE_VMEM = 40 * 1024 * 1024
PRODUCTS_VMEM = 24 * 1024 * 1024

epsilon = 1e-06


def split_bf16(value):
    high = value.astype(jnp.bfloat16)
    low = (value - high.astype(jnp.float32)).astype(jnp.bfloat16)
    return high, low


GROUP = 2


def gains_kernel(vis_hbm, mod_hbm, out_ref, vis, mod, *scratch, channels, intervals, rows):
    count = channels * intervals // GROUP
    matrices, powers, (first, arrived) = scratch[:count], scratch[count : 2 * count], scratch[2 * count :]
    zero = jnp.zeros((8, N), jnp.float32)

    def place(group, k):
        return divmod(group * GROUP + k, intervals)

    def fetch(group, k):
        c, t = place(group, k)
        return (
            pltpu.make_async_copy(vis_hbm.at[c, t], vis.at[c, t], arrived.at[0, c, t]),
            pltpu.make_async_copy(mod_hbm.at[c, t], mod.at[c, t], arrived.at[1, c, t]),
        )

    for group in range(count):
        for k in range(GROUP):
            for copy in fetch(group, k):
                copy.start()

    def build(group, k, start, sums):
        c, t = place(group, k)
        at = pl.ds(start, rows)
        vis_re = vis[c, t, 0, at, :].astype(jnp.float32)
        vis_im = vis[c, t, 1, at, :].astype(jnp.float32)
        mod_re = mod[c, t, 0, at, :].astype(jnp.float32)
        mod_im = mod[c, t, 1, at, :].astype(jnp.float32)
        parts = (
            mod_re * vis_re + mod_im * vis_im,
            mod_im * vis_re - mod_re * vis_im,
            mod_re * mod_re + mod_im * mod_im,
        )
        out = []
        for index, part in enumerate(parts):
            if index < 2:
                matrices[group][k, pl.ds(index * N + start, rows), :] = part.astype(jnp.bfloat16)
            else:
                powers[group][k, at, :] = part
            out.append(sums[index] + jnp.sum(part.reshape(rows // 8, 8, N), axis=0))
        return tuple(out)

    def first_gains(group, k, sums):
        num_re, num_im, power = (jnp.sum(part, axis=0, keepdims=True) for part in sums)
        power = power + epsilon
        first[group, k, 0:1, :] = num_re / power
        first[group, k, 1:2, :] = num_im / power

    def build_in_pieces(group):
        for k in range(GROUP):
            sums = (zero, zero, zero)
            for start in range(0, N, rows):
                sums = build(group, k, start, sums)
                if start + rows == N:
                    first_gains(group, k, sums)
                yield

    row = lax.broadcasted_iota(jnp.int32, (8, N), 0)

    def slab(*entries):
        value = jnp.zeros((8, N), jnp.float32)
        for position, entry in enumerate(entries):
            value = jnp.where(row == position, entry.astype(jnp.float32), value)
        return value.astype(jnp.bfloat16)

    def spread(gain_re, gain_im):
        magnitude = gain_re * gain_re + gain_im * gain_im
        return [
            jnp.broadcast_to(magnitude[:, i * BLK : (i + 1) * BLK], (BLK, BLK)).T for i in range(GROUPS)
        ]

    def products(group, k, gain, tiles):
        gain_re, gain_im = gain
        re_high, re_low = split_bf16(gain_re)
        im_high, im_low = split_bf16(gain_im)
        left = slab(re_high, re_low, im_high, im_low)
        right = slab(-im_high, -im_low, re_high, re_low)
        num = jnp.dot(
            jnp.concatenate([left, right], axis=1), matrices[group][k], preferred_element_type=jnp.float32
        )
        denominator = []
        for j in range(GROUPS):
            total = zero[:, :BLK]
            for i in range(GROUPS):
                block = powers[group][k, i * BLK : (i + 1) * BLK, j * BLK : (j + 1) * BLK]
                total = total + jnp.sum((block * tiles[i]).reshape(BLK // 8, 8, BLK), axis=0)
            denominator.append(jnp.sum(total, axis=0, keepdims=True))
        return num, jnp.concatenate(denominator, axis=1) + epsilon

    def update(index, gain, num, denominator):
        new_re = (num[0:1] + num[1:2]) / denominator
        new_im = (num[2:3] + num[3:4]) / denominator
        if index % 2 == 1:
            return 0.5 * (new_re + gain[0]), 0.5 * (new_im + gain[1])
        return new_re, new_im

    def iterate(group, beside):
        gains = [(first[group, k, 0:1, :], first[group, k, 1:2, :]) for k in range(GROUP)]
        tiles = [spread(*gain) for gain in gains]
        waiting = None
        for index in range(1, ITERS):
            for k in range(GROUP):
                found = products(group, k, gains[k], tiles[k])
                beside()
                if waiting is not None:
                    before, at, values = waiting
                    gains[at] = update(before, gains[at], *values)
                    tiles[at] = spread(*gains[at])
                waiting = (index, k, found)
        before, at, values = waiting
        gains[at] = update(before, gains[at], *values)
        return gains

    for k in range(GROUP):
        for copy in fetch(0, k):
            copy.wait()

        def chunk(index, sums, k=k):
            return build(0, k, pl.multiple_of(index * rows, rows), sums)

        first_gains(0, k, lax.fori_loop(0, N // rows, chunk, (zero, zero, zero), unroll=4))

    for group in range(count):
        later = iter(())
        if group + 1 < count:
            for k in range(GROUP):
                for copy in fetch(group + 1, k):
                    copy.wait()
            later = build_in_pieces(group + 1)
        share = -(-(N // rows) // (ITERS - 1))

        def beside():
            for _ in range(share):
                next(later, None)

        for k, (gain_re, gain_im) in enumerate(iterate(group, beside)):
            c, t = place(group, k)
            first_re = gain_re[:, :1]
            first_im = gain_im[:, :1]
            divisor = jnp.maximum(jnp.sqrt(first_re * first_re + first_im * first_im), 1.0)
            unit_re = first_re / divisor
            unit_im = -first_im / divisor
            out_ref[c, t, 0:1, :] = gain_re * unit_re - gain_im * unit_im
            out_ref[c, t, 1:2, :] = gain_re * unit_im + gain_im * unit_re


def referenced_gains(visibilities, model):
    channels, intervals = visibilities.shape[:2]
    there = pl.BlockSpec(memory_space=pltpu.HBM)
    return pl.pallas_call(
        functools.partial(gains_kernel, channels=channels, intervals=intervals, rows=32),
        in_specs=[there, there],
        out_specs=pl.BlockSpec(memory_space=pltpu.VMEM),
        out_shape=jax.ShapeDtypeStruct((channels, intervals, 2, N), jnp.float32),
        scratch_shapes=[
            pltpu.VMEM(visibilities.shape, jnp.bfloat16),
            pltpu.VMEM(model.shape, jnp.bfloat16),
        ]
        + [pltpu.VMEM((GROUP, 2 * N, N), jnp.bfloat16)] * (channels * intervals // GROUP)
        + [pltpu.VMEM((GROUP, N, N), jnp.float32)] * (channels * intervals // GROUP)
        + [
            pltpu.VMEM((channels * intervals // GROUP, GROUP, 8, N), jnp.float32),
            pltpu.SemaphoreType.DMA((2, channels, intervals)),
        ],
        compiler_params=pltpu.CompilerParams(vmem_limit_bytes=GAINS_VMEM),
        cost_estimate=pl.CostEstimate(
            flops=channels * intervals * N * N * 60, bytes_accessed=channels * intervals * N * N * 8, transcendentals=0
        ),
        name="gains",
    )(visibilities, model)


ROWS = (96, 96, 64)


PIECE = 32
PIECES = BLK // PIECE
CELLS = 2 * PIECES


def prepare_kernel(right_ref, table):
    for w in range(NWEIGHT):
        table[w * BLK : (w + 1) * BLK, :] = right_ref[w].astype(jnp.float32).T.astype(jnp.bfloat16)


def calibrate_kernel(
    weight_ref, target_ref, width_ref, place_ref,
    vis_hbm, mid_ref, low_ref, high_ref, left_ref, table, *refs, channels, intervals, all_intervals,
):
    send, keep = refs[:2]
    own_cells, refs = refs[2 : 2 + CELLS], refs[2 + CELLS :]
    cells, refs = refs[:CELLS], refs[CELLS:]
    vis, inverse, down_even, down_odd, arrived = refs[:5]
    steps = channels * intervals

    def fetch(step):
        return pltpu.make_async_copy(
            vis_hbm.at[step // intervals, step % intervals], vis.at[step], arrived.at[step]
        )

    for step in range(steps):
        fetch(step).start()

    def spread(at, down):
        for part in range(2):
            for i in range(GROUPS):
                span = slice(i * BLK, (i + 1) * BLK)
                down[part, span, :] = jnp.broadcast_to(inverse[at, part : part + 1, span], (BLK, BLK)).T

    for channel in range(channels):
        width = width_ref[channel]
        for interval in range(intervals):
            smooth = jnp.zeros((2, N), jnp.float32)
            count = jnp.float32(0)
            for offset in range(-HW, HW + 1):
                at = place_ref[0] + interval + offset
                inside = ((abs(offset) <= width) & (at >= 0) & (at < all_intervals)).astype(jnp.float32)
                spot = interval + offset
                if spot < 0:
                    value = low_ref[channel, spot + HW]
                elif spot >= intervals:
                    value = high_ref[channel, spot - intervals]
                else:
                    value = mid_ref[channel, spot]
                smooth = smooth + inside * value
                count = count + inside
            smooth = smooth / count
            squares = smooth * smooth
            denominator = jnp.maximum(squares[0:1] + squares[1:2], 1.0)
            at = channel * intervals + interval
            inverse[at, 0:1, :] = smooth[0:1] / denominator
            inverse[at, 1:2, :] = -smooth[1:2] / denominator
    for array in cells:
        array[...] = jnp.zeros_like(array)
    spread(0, down_even)

    def add_later(waiting):
        cell, piece, value_re, value_im = waiting
        cells[piece][cell] += value_re
        cells[PIECES + piece][cell] += value_im

    def calibrate(step, down, next_down):
        channel = step // intervals
        interval = step % intervals
        spread(jnp.minimum(step + 1, steps - 1), next_down)
        waiting = []
        for i in range(GROUPS):
            cell = [
                weight_ref[channel, block] * BANKS + target_ref[channel, interval * GROUPS * GROUPS + block]
                for block in range(i * GROUPS, (i + 1) * GROUPS)
            ]
            for j in range(GROUPS):
                span = slice(j * BLK, (j + 1) * BLK)
                for piece in range(PIECES):
                    at = slice(i * BLK + piece * PIECE, i * BLK + (piece + 1) * PIECE)
                    row_re = down[0, at, :]
                    row_im = down[1, at, :]
                    vis_re = vis[step, 0, at, span].astype(jnp.float32)
                    vis_im = vis[step, 1, at, span].astype(jnp.float32)
                    col_re = inverse[step, 0:1, span]
                    col_im = inverse[step, 1:2, span]
                    left_re = row_re * vis_re - row_im * vis_im
                    left_im = row_re * vis_im + row_im * vis_re
                    out_re = left_re * col_re + left_im * col_im
                    out_im = left_im * col_re - left_re * col_im
                    if len(waiting) == 3:
                        add_later(waiting.pop(0))
                    waiting.append((cell[j], piece, out_re, out_im))
        for entry in waiting:
            add_later(entry)

    def pair(turn, carry):
        step = 2 * turn
        fetch(step).wait()
        fetch(step + 1).wait()
        calibrate(step, down_even, down_odd)
        calibrate(step + 1, down_odd, down_even)
        return carry

    lax.fori_loop(0, steps // 2, pair, 0)
    four = BANKS // 2

    def cell_of(turn, w):
        own = w * BANKS + place_ref[3 + four + turn]
        for array, out in zip(cells, own_cells):
            out[w * four + turn] = array[own]
        return w * BANKS + place_ref[3 + turn]

    bank_products(place_ref, cells, cell_of, left_ref, table, send, keep, *refs[5:])


def own_products_kernel(place_ref, left_ref, table, *refs):
    def cell_of(turn, w):
        return w * (BANKS // 2) + turn

    bank_products(place_ref, refs[:CELLS], cell_of, left_ref, table, *refs[CELLS:])


def bank_products(
    place_ref, cells, cell_of, left_ref, table, send, keep, formed_even, formed_odd, product_even, product_odd
):
    count = BANKS // 2
    core = place_ref[1]
    across = place_ref[2]
    formed = (formed_even, formed_odd)
    product = (product_even, product_odd)

    def left_product(turn, w):
        cell = cell_of(turn, w)
        pair = jnp.concatenate(
            [
                jnp.concatenate([array[cell] for array in cells[:PIECES]], axis=0),
                jnp.concatenate([array[cell] for array in cells[PIECES:]], axis=0),
            ],
            axis=1,
        )
        high, low = split_bf16(pair)
        left = left_ref[w]
        beams = jnp.dot(
            jnp.concatenate([left, left], axis=1),
            jnp.concatenate([high, low], axis=0),
            preferred_element_type=jnp.float32,
        ).astype(jnp.bfloat16)
        formed[turn % 2][:BEAMS, w * BLK : (w + 1) * BLK] = beams[:, :BLK]
        formed[turn % 2][BEAMS:, w * BLK : (w + 1) * BLK] = beams[:, BLK:]

    def right_product(turn):
        product[turn % 2][...] = jnp.dot(
            formed[turn % 2][...], table[...], preferred_element_type=jnp.float32
        )

    def hand_out(turn):
        for part, out in ((1 - core, send), (core, keep)):
            start = 0
            for group, size in enumerate(rows // 2 for rows in ROWS):
                for away, half in ((0, across), (1, 1 - across)) if group < 2 else ((0, 0), (1, 1)):
                    at = part * BEAMS + start + half * size
                    out[turn, start + away * size : start + (away + 1) * size, :] = product[turn % 2][
                        pl.ds(pl.multiple_of(at, 16), size), :
                    ]
                start += 2 * size

    for turn in range(count + 1):
        if turn:
            right_product(turn - 1)
        if turn < count:
            for w in range(NWEIGHT):
                left_product(turn, w)
        if turn:
            hand_out(turn - 1)


SCALARS = pl.BlockSpec(memory_space=pltpu.SMEM)
VECTORS = pl.BlockSpec(memory_space=pltpu.VMEM)


def beam_products(weight_index, target_bank, widths, place, all_intervals, visibilities, mid, low, high, beam_left, beam_right):
    channels, intervals = visibilities.shape[:2]
    steps = channels * intervals
    table = pl.pallas_call(
        prepare_kernel,
        in_specs=[VECTORS],
        out_specs=VECTORS,
        out_shape=jax.ShapeDtypeStruct((NWEIGHT * BLK, BEAMS), jnp.bfloat16),
        compiler_params=pltpu.CompilerParams(vmem_limit_bytes=PREPARE_VMEM),
        cost_estimate=pl.CostEstimate(flops=10**6, bytes_accessed=1024 * 1024, transcendentals=0),
        name="prepare",
    )(lax.optimization_barrier((beam_right, mid))[0])
    banks_shape = [jax.ShapeDtypeStruct((BANKS // 2, BEAMS, BEAMS), jnp.float32)] * 2
    product_scratch = [pltpu.VMEM((2 * BEAMS, NWEIGHT * BLK), jnp.bfloat16)] * 2 + [
        pltpu.VMEM((2 * BEAMS, BEAMS), jnp.float32)
    ] * 2
    send_away, keep_away, *cells = pl.pallas_call(
        functools.partial(
            calibrate_kernel, channels=channels, intervals=intervals, all_intervals=all_intervals
        ),
        in_specs=[SCALARS] * 4 + [pl.BlockSpec(memory_space=pltpu.HBM)] + [VECTORS] * 5,
        out_specs=[VECTORS] * (2 + CELLS),
        scratch_shapes=[pltpu.VMEM((NWEIGHT * BANKS, PIECE, BLK), jnp.float32)] * CELLS
        + [
            pltpu.VMEM((steps, 2, N, N), jnp.bfloat16),
            pltpu.VMEM((steps, 8, N), jnp.float32),
            pltpu.VMEM((2, N, BLK), jnp.float32),
            pltpu.VMEM((2, N, BLK), jnp.float32),
            pltpu.SemaphoreType.DMA((steps,)),
        ]
        + product_scratch,
        out_shape=banks_shape
        + [jax.ShapeDtypeStruct((NWEIGHT * BANKS // 2, PIECE, BLK), jnp.float32)] * CELLS,
        compiler_params=pltpu.CompilerParams(vmem_limit_bytes=CALIBRATE_VMEM),
        cost_estimate=pl.CostEstimate(
            flops=2 * 10**9, bytes_accessed=steps * N * N * 8, transcendentals=0
        ),
        name="calibrate",
    )(
        weight_index, target_bank.reshape(channels, -1), widths, place,
        visibilities, mid, low, high, beam_left, table,
    )
    send_own, keep_own = pl.pallas_call(
        own_products_kernel,
        in_specs=[SCALARS] + [VECTORS] * (2 + CELLS),
        out_specs=[VECTORS] * 2,
        scratch_shapes=product_scratch,
        out_shape=banks_shape,
        compiler_params=pltpu.CompilerParams(vmem_limit_bytes=PRODUCTS_VMEM),
        cost_estimate=pl.CostEstimate(
            flops=2 * 10**9, bytes_accessed=2 * 1024 * 1024, transcendentals=0
        ),
        name="products",
    )(place, beam_left, table, *cells)
    return send_away, keep_away, send_own, keep_own


SLOTS = tuple((1 - (p >> 2)) | ((p & 3) << 1) for p in range(BANKS))


def swap(value, axis, mask):
    count = lax.axis_size(axis)
    return lax.ppermute(value, axis, [(i, i ^ mask) for i in range(count)])


def assemble_kernel(place_ref, mine, other, out):
    core = place_ref[1]
    across = place_ref[2]
    half_p, half_q = ROWS[0] // 2, ROWS[1] // 2
    for part, rows in ((core, mine), (1 - core, other)):
        base = part * BEAMS
        start = 0
        for half in (across, 1 - across):
            for at, size in ((0, half_p), (ROWS[0], half_q)):
                out[pl.ds(pl.multiple_of(base + at + half * size, 16), size), :] = rows[start : start + size, :]
                start += size
        out[pl.ds(pl.multiple_of(base + start, 16), ROWS[2]), :] = rows[start:, :]


def reduce_banks(place, send_away, keep_away, send_own, keep_own):
    four = BANKS // 2
    half_p, half_q = ROWS[0] // 2, ROWS[1] // 2
    q_at = 2 * half_p
    q_half = q_at + half_q
    r_at = q_half + half_q
    got_away = swap(send_away, "tm", 1)
    got_own = swap(send_own, "tm", 1)

    def away(low, high):
        return keep_away[:, low:high] + got_away[:, low:high]

    def own(low, high):
        return keep_own[:, low:high] + got_own[:, low:high]

    p_got = swap(away(0, q_at), "chan", 1)
    q_got = swap(jnp.concatenate([away(q_half, r_at), own(q_half, r_at)], axis=0), "tm", 2)
    r_here = jnp.stack([own(r_at, None), away(r_at, None)], axis=1)
    r_got = [swap(r_here[k], "chan", 2 * k) for k in (3, 2, 1)]
    p_here = own(0, q_at) + p_got
    p_got = swap(p_here[:, half_p:], "tm", 2)
    p_got, *r_got = lax.optimization_barrier((p_got, *r_got))
    p_here = p_here[:, :half_p] + p_got
    q_own = own(q_at, q_half) + q_got[four:]
    q_other = away(q_at, q_half) + q_got[:four]
    q_here = q_own + swap(q_other, "chan", 1)
    r_here = r_here[0] + r_got[0] + r_got[1] + r_got[2]
    r_here = r_here[0] + swap(r_here[1], "chan", 1)
    here = jnp.concatenate([p_here, q_here], axis=1)
    z_got = [swap(here[k], "chan", 2 * k) for k in (3, 2, 1)]
    here = here[0] + z_got[0] + z_got[1] + z_got[2]
    r_here = r_here + swap(r_here, "tm", 2)
    mine = jnp.concatenate([here, swap(here, "tm", 2), r_here], axis=0)
    other = swap(mine, "tm", 1)
    return pl.pallas_call(
        assemble_kernel,
        in_specs=[SCALARS, VECTORS, VECTORS],
        out_specs=VECTORS,
        out_shape=jax.ShapeDtypeStruct((2 * BEAMS, BEAMS), jnp.float32),
        compiler_params=pltpu.CompilerParams(vmem_limit_bytes=PREPARE_VMEM),
        name="assemble",
    )(place, mine, other)


def reduce_plain(send_first, keep_first, send_last, keep_last):
    keep = jnp.concatenate([keep_first, keep_last])
    send = jnp.concatenate([send_first, send_last])
    banks = jnp.stack([keep, send], axis=1).reshape((BANKS * 2 * BEAMS, BEAMS))
    shares = lax.psum_scatter(banks, "chan", scatter_dimension=0, tiled=True)
    return lax.psum(shares, "tm")


def neighbour_gains(gains):
    count = lax.axis_size("tm")
    odd = lax.axis_index("tm") % 2 == 1
    head = gains[:, :HW]
    tail = gains[:, gains.shape[1] - HW :]
    inner = lax.ppermute(jnp.where(odd, head, tail), "tm", [(i, i ^ 1) for i in range(count)])
    links = [(i, i + 1) for i in range(1, count - 1, 2)]
    outer = lax.ppermute(jnp.where(odd, tail, head), "tm", links + [(j, i) for i, j in links])
    return jnp.where(odd, inner, outer), jnp.where(odd, outer, inner)


def local(visibilities, model, beam_left, beam_right, weight_index, target_bank, widths):
    local_intervals = visibilities.shape[1]
    count = lax.axis_size("tm")
    tm = lax.axis_index("tm")
    chan = lax.axis_index("chan")
    one_bank_each = lax.axis_size("chan") == BANKS and count == 4
    if one_bank_each:
        place = [tm * local_intervals, tm % 2, tm // 2] + [chan ^ slot for slot in SLOTS]
    else:
        place = [tm * local_intervals, 0, 0] + list(range(BANKS))
    place = jnp.stack([jnp.asarray(entry, jnp.int32) for entry in place])
    gains = referenced_gains(visibilities, model)
    low, high = neighbour_gains(gains)
    pieces = beam_products(
        weight_index, target_bank, widths, place, count * local_intervals,
        visibilities, gains, low, high, beam_left, beam_right,
    )
    if one_bank_each:
        return reduce_banks(place, *pieces)
    return reduce_plain(*pieces)


def solution(mesh):
    return jax.shard_map(
        local,
        mesh=mesh,
        in_specs=(
            P("chan", "tm", None, None, None),
            P("chan", "tm", None, None, None),
            P(),
            P(),
            P("chan", None),
            P("chan", "tm", None),
            P("chan"),
        ),
        out_specs=P("chan", None),
        check_vma=False,
    )
```
